32 devices in a mesh: group: 2 (over y), op: 4 (over z), site: 2 (over x), blk: 2 (over core).
Axes of the slice: x: 2, y: 2, z: 4, core: 2. Of those that a mesh axis runs over, the one named last changes fastest.
Arguments:
- psi: bfloat16 [4, 256, 2048], P(('group', 'site'), 'blk'), parts along dimension 0, may hold values from -6 to 6
- right_ops: bfloat16 [4, 8, 8, 256, 256], P(('group', 'site'), 'op'), parts along dimension 0
- left_blocks: bfloat16 [4, 8, 4, 8, 64, 64], P(('group', 'site'), 'op', 'blk'), parts along dimension 0
- sources: int32 [4, 8, 4, 8], P(('group', 'site'), 'op', 'blk'), parts along dimension 0, may hold values from 0 to 3
- env_basis: bfloat16 [4, 2048, 256], P(('group', 'site')), parts along dimension 0, may hold values from -0.125 to 0.125
Outputs:
- amplitudes: bfloat16 [4, 256, 2048], P(('group', 'site'), 'blk'), parts along dimension 0
- environment: float32 [4, 256, 256], P(('group', 'site'), 'blk'), parts along dimension 0
The draws below stay inside these ranges and needn't reach their ends.
There are 2 independent parts, one for each index of `group`. The reference program is written for one: setup_inputs(seed, part) draws one part's arguments, and reference() takes and returns one part's arrays. A program takes and returns all parts, laid end to end along the dimension named above; each array names one. Nothing has to cross between parts.
All inputs are finite; a program needn't handle non-finite values.
Results may differ from the reference program's by a relative error of at most 0.012.
Values may be sent and summed in bfloat16 or wider, within the bound.
A program may use at most 64 MiB of HBM per device.

```python
import jax
import jax.numpy as jnp
from jax import lax

BS = 64
C = 2048
RB = 256
NNZ = 8
ITERS = 3
NBLK = 4
ROWS = 256
TERMS = 8
SEGS = 2


def draw_right_ops(key, part):
    key = jax.random.fold_in(key, 11)
    nrb = C // RB
    base = jax.random.normal(key, (SEGS, TERMS, nrb, RB, RB), jnp.float32)
    spread = 2.5
    place = jnp.arange(nrb, dtype=jnp.float32) / max(nrb - 1, 1) - 0.5
    scale = jnp.exp(jnp.log(spread) * place)
    return (base * scale[None, None, :, None, None] * RB ** (-0.5)).astype(jnp.bfloat16)


def draw_left_blocks(key, part):
    key = jax.random.fold_in(key, 23)
    base = jax.random.normal(key, (SEGS, TERMS, NBLK, NNZ, BS, BS), jnp.float32)
    spread = 4.0
    place = jnp.arange(NBLK, dtype=jnp.float32) / max(NBLK - 1, 1) - 0.5
    scale = jnp.exp(jnp.log(spread) * place)
    return (base * scale[None, None, :, None, None, None] * (NNZ * BS) ** (-0.5)).astype(jnp.bfloat16)


def set_ends(drawn, key, low, largest):
    index_at = [jax.random.randint(jax.random.fold_in(key, axis), (), 0, length) for axis, length in enumerate(drawn.shape)]
    longest = drawn.shape.index(max(drawn.shape))
    beside = index_at[:longest] + [(index_at[longest] + 1) % drawn.shape[longest]] + index_at[longest + 1:]
    return drawn.at[tuple(index_at)].set(low).at[tuple(beside)].set(largest)


def steps_of(own_key, extent, cuts, low, top_value):
    factor_of, own = 1.0, jax.random.fold_in(own_key, 6)
    for dim, shards_of in cuts:
        heights = jnp.exp(jax.random.uniform(jax.random.fold_in(own, dim), (shards_of,), jnp.float32, low / len(cuts), top_value / len(cuts)))
        factor_of = factor_of * jnp.repeat(heights, extent[dim] // shards_of).reshape([-1 if axis == dim else 1 for axis in range(len(extent))])
    return factor_of


def scatter_about(key, shape, scale, most, shards=(), kind=jnp.bfloat16):
    values = jax.random.normal(key, shape, jnp.float32) * scale
    if len(shards) > 0:
        values = steps_of(key, shape, shards, -0.22, 0.18) * values
    return jnp.clip(values, min=-most, max=most).astype(kind)


def setup_inputs(seed: int = 0, part: int = 0) -> dict:
    splits = jax.random.split(jax.random.key(seed), 6)
    own_keys = jax.random.split(jax.random.fold_in(splits[5], part), 6)
    return {
        "psi": scatter_about(own_keys[0], (SEGS, ROWS, C), 1.0, 6.0, ((0, 2), (1, 2))),
        "right_ops": draw_right_ops(jax.random.fold_in(jax.random.fold_in(splits[5], part), 71), part),
        "left_blocks": draw_left_blocks(jax.random.fold_in(jax.random.fold_in(splits[5], part), 71), part),
        "sources": set_ends(jax.random.randint(own_keys[3], (SEGS, TERMS, NBLK, NNZ), 0, NBLK), jax.random.fold_in(own_keys[3], 1), 0, NBLK - 1).astype(jnp.int32),
        "env_basis": scatter_about(own_keys[4], (SEGS, C, ROWS), C ** -0.5, 0.125, ((0, 2),)),
    }


def apply_terms(vector, right_seg, left_seg, source_seg):
    rows, cols = vector.shape
    nrb, rblock = (right_seg.shape[1], right_seg.shape[2])
    bsize = left_seg.shape[-1]
    nblocks = rows // bsize

    def one_term(total, pieces):
        right_blocks, left_part, source_part = pieces
        split = vector.astype(jnp.float32).reshape(rows, nrb, rblock)
        moved = jnp.einsum('ikb,kbc->ikc', split, right_blocks.astype(jnp.float32))
        moved = moved.reshape(rows, cols).astype(jnp.bfloat16)
        stacked = moved.reshape(nblocks, bsize, cols)
        picked = stacked[source_part.astype(jnp.int32)]
        image = jnp.einsum('djab,djbc->dac', left_part.astype(jnp.float32), picked.astype(jnp.float32))
        return (total + image.reshape(rows, cols), None)
    start = jnp.zeros((rows, cols), jnp.float32)
    total, unused = lax.scan(one_term, start, (right_seg, left_seg, source_seg))
    return total

def reference(psi, right_ops, left_blocks, sources, env_basis):
    segments = psi.shape[0]
    rows, cols = (psi.shape[1], psi.shape[2])
    count = float(rows * cols)
    outputs = []
    factors = []
    for segment in range(segments):
        vector = psi[segment]
        for step in range(ITERS):
            image = apply_terms(vector, right_ops[segment], left_blocks[segment], sources[segment])
            inner_ww = jnp.sum(image * image)
            vector = (image * jnp.sqrt(count / inner_ww)).astype(jnp.bfloat16)
        outputs.append(vector)
        factor = jnp.dot(vector, env_basis[segment], preferred_element_type=jnp.float32)
        factor = factor * jnp.sqrt(float(rows * rows) / jnp.sum(factor * factor))
        factors.append(factor)
    carried = jnp.eye(rows, dtype=jnp.float32)
    environs = []
    for segment in range(segments):
        if segment == 0:
            environs.append(carried)
        else:
            environs.append(carried * lax.rsqrt(jnp.mean(carried * carried)))
        carried = jnp.dot(carried, factors[segment], precision=lax.Precision.HIGHEST, preferred_element_type=jnp.float32)
    return (jnp.stack(outputs), jnp.stack(environs))
```

```python
import functools

import jax
import jax.numpy as jnp
from jax import lax
from jax.experimental import pallas as pl
from jax.experimental.pallas import tpu as pltpu
from jax.sharding import PartitionSpec as P

ITERS = 3
MESH = pl.DeviceIdType.MESH
F32 = jnp.float32
BF16 = jnp.bfloat16


def entering(value, axis, combine, identity):
    size, here = (lax.axis_size(axis), lax.axis_index(axis))
    everything = lax.all_gather(value.astype(jnp.bfloat16), axis)
    start = jnp.broadcast_to(jnp.asarray(identity, value.dtype), value.shape)

    def lap(k, before):
        reached = k < here
        new = combine(before, everything[k].astype(value.dtype))
        return jnp.where(reached, new, before)

    return lax.fori_loop(0, size, lap, start)


def chain_product(first, second):
    return jnp.dot(
        first, second, precision=lax.Precision.HIGHEST, preferred_element_type=jnp.float32
    )


def pick_rows(table, index):
    return table[index]


def local_terms(vector, right_seg, left_seg, source_seg):
    local_rows, cols = vector.shape
    nrb, rblock = (right_seg.shape[1], right_seg.shape[2])
    bsize = left_seg.shape[-1]
    split = vector.reshape(local_rows, nrb, rblock)
    moved = jnp.einsum("ikb,tkbc->tikc", split, right_seg, preferred_element_type=jnp.float32)
    moved = moved.reshape(right_seg.shape[0], local_rows, cols).astype(jnp.bfloat16)
    gathered = lax.all_gather(moved, "blk", axis=1, tiled=True)
    stacked = gathered.reshape(gathered.shape[0], gathered.shape[1] // bsize, bsize, cols)
    picked = jax.vmap(pick_rows)(stacked, source_seg)
    image = jnp.einsum("tdjab,tdjbc->dac", left_seg, picked, preferred_element_type=jnp.float32)
    return image.reshape(local_rows, cols)


def general_plan(psi, right_ops, left_blocks, sources, env_basis):
    local_rows, cols = (psi.shape[1], psi.shape[2])
    count = float(local_rows * lax.axis_size("blk") * cols)
    vector = psi[0]
    for step in range(ITERS):
        partial_sum = local_terms(vector, right_ops[0], left_blocks[0], sources[0])
        image = lax.psum(partial_sum, "op")
        inner_ww = lax.psum(jnp.sum(image * image), "blk")
        vector = (image * jnp.sqrt(count / inner_ww)).astype(jnp.bfloat16)
    factor_rows = jnp.dot(vector, env_basis[0], preferred_element_type=jnp.float32)
    factor = lax.all_gather(factor_rows.astype(jnp.bfloat16), "blk", axis=0, tiled=True).astype(
        factor_rows.dtype
    )
    total_rows = factor.shape[1]
    factor = factor * jnp.sqrt(float(total_rows * total_rows) / jnp.sum(factor * factor))
    identity = jnp.eye(total_rows, dtype=jnp.float32)
    carried = entering(factor, "site", chain_product, identity)
    scaled = carried * lax.rsqrt(jnp.mean(carried * carried))
    settled = jnp.where(lax.axis_index("site") == 0, carried, scaled)
    mine = lax.dynamic_slice_in_dim(settled, lax.axis_index("blk") * local_rows, local_rows, 0)
    return (vector[None], mine[None])


def column_kernel(
    n, src_ref, psi_ref, right_ref, left_ref, env_ref, amp_ref, out_ref,
    r_all, l_all, vec, env, tail, meta, fac, fac_in, fmeta,
    local_sem, r_send, r_recv, p_send, p_recv, l_send, l_recv, s_send, s_recv,
    a_send, a_recv, x_send, x_recv, m_send, m_recv, f_send, f_recv, g_send, g_recv,
):
    terms, nrb, rb, _ = right_ref.shape
    rows, cols = psi_ref.shape
    nd, nnz, bs = left_ref.shape[1], left_ref.shape[2], left_ref.shape[3]
    all_rows = 2 * rows
    z = lax.axis_index("op")
    c = lax.axis_index("blk")
    site = lax.axis_index("site")
    k = 2 * z + c
    ksib = 2 * z + 1 - c
    mine = pl.ds(pl.multiple_of(c * rows, rows), rows)
    theirs = pl.ds(pl.multiple_of((1 - c) * rows, rows), rows)

    def remote(src, dst, send, recv, device):
        return pltpu.make_async_remote_copy(
            src_ref=src, dst_ref=dst, send_sem=send, recv_sem=recv,
            device_id=device, device_id_type=MESH,
        )

    sibling = {"blk": 1 - c}
    across = {"site": 1 - site}
    diagonal = {"site": 1 - site, "blk": 1 - c}

    own_r = pltpu.make_async_copy(right_ref.at[:, k], r_all.at[z], local_sem.at[0])
    own_p = pltpu.make_async_copy(
        psi_ref.at[:, pl.ds(pl.multiple_of(k * rb, rb), rb)], vec.at[mine], local_sem.at[1]
    )
    own_e = pltpu.make_async_copy(env_ref, env, local_sem.at[2])
    own_r.start()
    own_p.start()
    own_e.start()

    barrier = pltpu.get_barrier_semaphore()
    for off in range(1, n):
        pl.semaphore_signal(
            barrier, inc=1, device_id={"op": lax.rem(z + off, n)}, device_id_type=MESH
        )
    for dev in (sibling, across, diagonal):
        pl.semaphore_signal(barrier, inc=1, device_id=dev, device_id_type=MESH)
    pl.semaphore_wait(barrier, n + 2)

    def r_copy(off):
        dest = lax.rem(z + off, n)
        return remote(
            right_ref.at[:, 2 * dest + c], r_all.at[z], r_send.at[off], r_recv.at[z],
            {"op": dest},
        )

    order = sorted(range(1, n), key=lambda o: -min(o, n - o))
    for off in order:
        r_copy(off).start()
    p_copy = remote(
        psi_ref.at[:, pl.ds(pl.multiple_of(ksib * rb, rb), rb)], vec.at[mine],
        p_send, p_recv, sibling,
    )
    p_copy.start()

    diff = lax.broadcasted_iota(jnp.int32, (bs, all_rows), 1) - lax.broadcasted_iota(
        jnp.int32, (bs, all_rows), 0
    )
    for t in range(terms):
        for d in range(nd):
            total = jnp.zeros((bs, all_rows), F32)
            for j in range(nnz):
                place = jnp.where(diff == bs * src_ref[t, d, j], 1.0, 0.0).astype(BF16)
                total += jnp.dot(left_ref[t, d, j], place, preferred_element_type=F32)
            at = pl.ds(pl.multiple_of(c * rows + d * bs, bs), bs)
            l_all[z, t, at, :] = total.astype(BF16)

    def right_hop(ref, origin, send, recv):
        return remote(ref(origin), ref(origin), send, recv.at[origin], {"op": lax.rem(z + 1, n)})

    def left_hop(ref, origin, send, recv):
        return remote(
            ref(origin), ref(origin), send, recv.at[origin], {"op": lax.rem(z + n - 1, n)}
        )

    def start_line(ref, send, recv):
        @pl.when(z + 1 < n)
        def _():
            right_hop(ref, z, send.at[0, 0], recv).start()

        @pl.when(z > 0)
        def _():
            left_hop(ref, z, send.at[1, 0], recv).start()

    def step_line(ref, send, recv, s, use):
        @pl.when(z - s >= 0)
        def _():
            o = lax.rem(z - s + n, n)
            right_hop(ref, o, send.at[0, 0], recv).wait_recv()
            if s < n - 1:
                @pl.when(z + 1 < n)
                def _():
                    right_hop(ref, o, send.at[0, s], recv).start()
            use(o)

        @pl.when(z + s < n)
        def _():
            o = lax.rem(z + s, n)
            left_hop(ref, o, send.at[1, 0], recv).wait_recv()
            if s < n - 1:
                @pl.when(z > 0)
                def _():
                    left_hop(ref, o, send.at[1, s], recv).start()
            use(o)

    def end_line(ref, send, recv):
        for s in range(n - 1):
            @pl.when((z + 1 < n) & (z - s >= 0))
            def _():
                right_hop(ref, lax.rem(z - s + n, n), send.at[0, s], recv).wait_send()

            @pl.when((z > 0) & (z + s < n))
            def _():
                left_hop(ref, lax.rem(z + s, n), send.at[1, s], recv).wait_send()

    def l_slot(o):
        return l_all.at[o, :, mine, :]

    def to_sibling(o):
        return remote(l_slot(o), l_slot(o), s_send.at[o], s_recv.at[o], sibling)

    start_line(l_slot, l_send, l_recv)
    to_sibling(z).start()

    own_p.wait()
    p_copy.wait()
    own_r.wait()

    for s in range(1, n):
        step_line(l_slot, l_send, l_recv, s, lambda o: to_sibling(o).start())

    def product(o, start):
        v = vec[...]
        total = start
        for t in range(terms):
            moved = jnp.dot(v, r_all[o, t], preferred_element_type=F32).astype(BF16)
            total = total + jnp.dot(l_all[o, t], moved, preferred_element_type=F32)
        return total

    image = jnp.zeros((all_rows, rb), F32)
    for off in [0] + order[::-1]:
        o = lax.rem(z + off, n)
        to_sibling(o).wait_recv()
        if off:
            remote(
                right_ref.at[:, k], r_all.at[o], r_send.at[0], r_recv.at[o], {"op": o}
            ).wait_recv()
        image = product(o, image)

    exponent = jnp.zeros((1, 1), F32)

    def settle(image, exponent):
        top = jnp.max(jnp.abs(image), axis=(0, 1), keepdims=True)
        e = jnp.where(top > 0.0, jnp.clip(jnp.floor(jnp.log2(top)), -100.0, 100.0), 0.0)
        return image * jnp.exp2(-e), exponent + e

    for step in range(1, ITERS):
        image, exponent = settle(image, exponent)
        vec[...] = image.astype(BF16)
        image = jnp.zeros((all_rows, rb), F32)
        for o in range(n):
            image = product(o, image)
    image, exponent = settle(image, exponent)
    square = jnp.sum(image * image, axis=(0, 1), keepdims=True)
    vec[...] = image.astype(BF16)

    here = pl.ds(pl.multiple_of(c * rb, rb), rb)
    x_copy = remote(
        vec.at[theirs, :], tail.at[z, :, here], x_send.at[0], x_recv.at[0], sibling
    )
    x_copy.start()
    lane = lax.broadcasted_iota(jnp.int32, (8, 128), 1)
    meta[z, c] = jnp.where(lane == 0, jnp.broadcast_to(exponent, (8, 128)),
                           jnp.broadcast_to(square, (8, 128)))
    xm_copy = remote(meta.at[z, c], meta.at[z, c], x_send.at[1], x_recv.at[1], sibling)
    xm_copy.start()
    tail[z, :, here] = vec[mine, :]

    def a_slot(o):
        return tail.at[o]

    x_copy.wait()
    start_line(a_slot, a_send, a_recv)
    xm_copy.wait()

    def m_copy(off):
        return remote(
            meta.at[z], meta.at[z], m_send.at[off], m_recv.at[z], {"op": lax.rem(z + off, n)}
        )

    for off in range(1, n):
        m_copy(off).start()

    step_line(a_slot, a_send, a_recv, 1, lambda o: None)
    for off in range(1, n):
        o = lax.rem(z + off, n)
        remote(
            meta.at[o], meta.at[o], m_send.at[0], m_recv.at[o], {"op": o}
        ).wait_recv()

    exps = [meta[o // 2, o % 2][0:1, 0:1] for o in range(2 * n)]
    sqs = [meta[o // 2, o % 2][0:1, 1:2] for o in range(2 * n)]
    low = jnp.full((1, 1), -1.0e4, F32)
    big = low
    for e, q in zip(exps, sqs):
        big = jnp.maximum(big, jnp.where(q > 0.0, e, low))
    ww = jnp.zeros((1, 1), F32)
    rel = []
    for e, q in zip(exps, sqs):
        r = jnp.where(q > 0.0, jnp.exp2(jnp.maximum(e - big, -120.0)), 0.0)
        rel.append(r)
        ww = ww + q * r * r
    unit = jnp.sqrt(float(all_rows * cols) / ww)

    def finish(o, factor):
        for half in range(2):
            scale = rel[2 * o + half] * unit
            block = (tail[o, :, half * rb:(half + 1) * rb].astype(F32) * scale).astype(BF16)
            lo = (2 * o + half) * rb
            amp_ref[:, lo:lo + rb] = block
            factor = factor + jnp.dot(block, env[lo:lo + rb, :], preferred_element_type=F32)
        return factor

    for s in range(2, n):
        step_line(a_slot, a_send, a_recv, s, lambda o: None)
    own_e.wait()
    factor = jnp.zeros(out_ref.shape, F32)
    for o in range(n):
        factor = finish(o, factor)

    fac[...] = factor.astype(BF16)
    f_copy = remote(fac, fac_in, f_send, f_recv, across)
    f_copy.start()
    rounded = fac[...].astype(F32)
    fsq = jnp.sum(rounded * rounded, axis=(0, 1), keepdims=True)
    fmeta[0] = jnp.broadcast_to(fsq, (8, 128))
    g_near = remote(fmeta.at[0], fmeta.at[1], g_send.at[0], g_recv.at[0], across)
    g_far = remote(fmeta.at[0], fmeta.at[2], g_send.at[1], g_recv.at[1], diagonal)
    g_near.start()
    g_far.start()

    for off in range(1, n):
        r_copy(off).wait_send()
        m_copy(off).wait_send()
    end_line(l_slot, l_send, l_recv)
    end_line(a_slot, a_send, a_recv)
    for o in range(n):
        to_sibling(o).wait_send()
    g_near.wait()
    g_far.wait()
    f_copy.wait()
    total = fmeta[1][0:1, 0:1] + fmeta[2][0:1, 0:1]
    earlier = fac_in[...].astype(F32) * lax.rsqrt(total / float(all_rows * out_ref.shape[1]))
    eye = jnp.where(
        lax.broadcasted_iota(jnp.int32, out_ref.shape, 0) + c * rows
        == lax.broadcasted_iota(jnp.int32, out_ref.shape, 1), 1.0, 0.0,
    )
    first = jnp.full(out_ref.shape, site, jnp.int32) == 0
    out_ref[...] = jnp.where(first, eye, earlier)


def column_plan(psi, right_ops, left_blocks, sources, env_basis):
    n = lax.axis_size("op")
    rows, cols = psi.shape[1], psi.shape[2]
    terms, nrb, rb = right_ops.shape[1], right_ops.shape[2], right_ops.shape[3]
    width = env_basis.shape[2]
    dma = pltpu.SemaphoreType.DMA
    hbm = pl.BlockSpec(memory_space=pl.ANY)
    vmem = pl.BlockSpec(memory_space=pltpu.VMEM)
    amplitudes, environment = pl.pallas_call(
        functools.partial(column_kernel, n),
        out_shape=(
            jax.ShapeDtypeStruct((rows, cols), BF16),
            jax.ShapeDtypeStruct((rows, width), F32),
        ),
        in_specs=[pl.BlockSpec(memory_space=pltpu.SMEM), hbm, hbm, vmem, hbm],
        out_specs=(vmem, vmem),
        scratch_shapes=[
            pltpu.VMEM((n, terms, rb, rb), BF16),
            pltpu.VMEM((n, terms, 2 * rows, 2 * rows), BF16),
            pltpu.VMEM((2 * rows, rb), BF16),
            pltpu.VMEM((cols, width), BF16),
            pltpu.VMEM((n, rows, 2 * rb), BF16),
            pltpu.VMEM((n, 2, 8, 128), F32),
            pltpu.VMEM((rows, width), BF16),
            pltpu.VMEM((rows, width), BF16),
            pltpu.VMEM((3, 8, 128), F32),
            dma((3,)),
            dma((n,)), dma((n,)), dma, dma, dma((2, n)), dma((n,)), dma((n,)), dma((n,)),
            dma((2, n)), dma((n,)), dma((2,)), dma((2,)), dma((n,)), dma((n,)),
            dma, dma, dma((2,)), dma((2,)),
        ],
        compiler_params=pltpu.CompilerParams(
            collective_id=0, has_side_effects=True, vmem_limit_bytes=40 * 1024 * 1024
        ),
    )(sources[0], psi[0], right_ops[0], left_blocks[0], env_basis[0])
    return (amplitudes[None], environment[None])


def on_device(psi, right_ops, left_blocks, sources, env_basis):
    owners = lax.axis_size("op") * lax.axis_size("blk")
    fits = (
        owners == right_ops.shape[2]
        and lax.axis_size("blk") == 2
        and lax.axis_size("site") == 2
        and psi.shape[0] == 1
        and env_basis.shape[2] == 2 * psi.shape[1]
    )
    plan = column_plan if fits else general_plan
    return plan(psi, right_ops, left_blocks, sources, env_basis)


def solution(mesh):
    placed = (
        P(("group", "site"), "blk", None),
        P(("group", "site"), "op", None, None, None),
        P(("group", "site"), "op", "blk", None, None, None),
        P(("group", "site"), "op", "blk", None),
        P(("group", "site"), None, None),
    )
    return jax.shard_map(
        on_device,
        mesh=mesh,
        in_specs=placed,
        out_specs=(P(("group", "site"), "blk", None), P(("group", "site"), "blk", None)),
        check_vma=False,
    )
```

```python
import functools

import jax
import jax.numpy as jnp
from jax import lax
from jax.experimental import pallas as pl
from jax.experimental.pallas import tpu as pltpu
from jax.sharding import PartitionSpec as P

ITERS = 3
MESH = pl.DeviceIdType.MESH
F32 = jnp.float32
BF16 = jnp.bfloat16


def entering(value, axis, combine, identity):
    size, here = (lax.axis_size(axis), lax.axis_index(axis))
    everything = lax.all_gather(value.astype(jnp.bfloat16), axis)
    start = jnp.broadcast_to(jnp.asarray(identity, value.dtype), value.shape)

    def lap(k, before):
        reached = k < here
        new = combine(before, everything[k].astype(value.dtype))
        return jnp.where(reached, new, before)

    return lax.fori_loop(0, size, lap, start)


def chain_product(first, second):
    return jnp.dot(
        first, second, precision=lax.Precision.HIGHEST, preferred_element_type=jnp.float32
    )


def pick_rows(table, index):
    return table[index]


def local_terms(vector, right_seg, left_seg, source_seg):
    local_rows, cols = vector.shape
    nrb, rblock = (right_seg.shape[1], right_seg.shape[2])
    bsize = left_seg.shape[-1]
    split = vector.reshape(local_rows, nrb, rblock)
    moved = jnp.einsum("ikb,tkbc->tikc", split, right_seg, preferred_element_type=jnp.float32)
    moved = moved.reshape(right_seg.shape[0], local_rows, cols).astype(jnp.bfloat16)
    gathered = lax.all_gather(moved, "blk", axis=1, tiled=True)
    stacked = gathered.reshape(gathered.shape[0], gathered.shape[1] // bsize, bsize, cols)
    picked = jax.vmap(pick_rows)(stacked, source_seg)
    image = jnp.einsum("tdjab,tdjbc->dac", left_seg, picked, preferred_element_type=jnp.float32)
    return image.reshape(local_rows, cols)


def general_plan(psi, right_ops, left_blocks, sources, env_basis):
    local_rows, cols = (psi.shape[1], psi.shape[2])
    count = float(local_rows * lax.axis_size("blk") * cols)
    vector = psi[0]
    for step in range(ITERS):
        partial_sum = local_terms(vector, right_ops[0], left_blocks[0], sources[0])
        image = lax.psum(partial_sum, "op")
        inner_ww = lax.psum(jnp.sum(image * image), "blk")
        vector = (image * jnp.sqrt(count / inner_ww)).astype(jnp.bfloat16)
    factor_rows = jnp.dot(vector, env_basis[0], preferred_element_type=jnp.float32)
    factor = lax.all_gather(factor_rows.astype(jnp.bfloat16), "blk", axis=0, tiled=True).astype(
        factor_rows.dtype
    )
    total_rows = factor.shape[1]
    factor = factor * jnp.sqrt(float(total_rows * total_rows) / jnp.sum(factor * factor))
    identity = jnp.eye(total_rows, dtype=jnp.float32)
    carried = entering(factor, "site", chain_product, identity)
    scaled = carried * lax.rsqrt(jnp.mean(carried * carried))
    settled = jnp.where(lax.axis_index("site") == 0, carried, scaled)
    mine = lax.dynamic_slice_in_dim(settled, lax.axis_index("blk") * local_rows, local_rows, 0)
    return (vector[None], mine[None])


def column_kernel(
    n, src_ref, psi_ref, right_ref, left_ref, env_ref, amp_ref, out_ref,
    r_all, l_all, vec, env, left, tail, meta, rel, total_fac, fac, fac_in, fmeta,
    local_sem, r_send, r_recv, p_send, p_recv, l_send, l_recv, s_send, s_recv,
    a_send, a_recv, x_send, x_recv, m_send, m_recv, f_send, f_recv, g_send, g_recv,
):
    terms, nrb, rb, _ = right_ref.shape
    rows, cols = psi_ref.shape
    nd, nnz, bs = left_ref.shape[1], left_ref.shape[2], left_ref.shape[3]
    all_rows = 2 * rows
    z = lax.axis_index("op")
    c = lax.axis_index("blk")
    site = lax.axis_index("site")
    k = 2 * z + c
    ksib = 2 * z + 1 - c
    mine = pl.ds(pl.multiple_of(c * rows, rows), rows)
    theirs = pl.ds(pl.multiple_of((1 - c) * rows, rows), rows)

    def remote(src, dst, send, recv, device):
        return pltpu.make_async_remote_copy(
            src_ref=src, dst_ref=dst, send_sem=send, recv_sem=recv,
            device_id=device, device_id_type=MESH,
        )

    sibling = {"blk": 1 - c}
    across = {"site": 1 - site}
    diagonal = {"site": 1 - site, "blk": 1 - c}

    barrier = pltpu.get_barrier_semaphore()
    for off in range(1, n):
        pl.semaphore_signal(
            barrier, inc=1, device_id={"op": lax.rem(z + off, n)}, device_id_type=MESH
        )
    for dev in (sibling, across, diagonal):
        pl.semaphore_signal(barrier, inc=1, device_id=dev, device_id_type=MESH)

    own_l = pltpu.make_async_copy(left_ref, left, local_sem.at[3])
    own_p = pltpu.make_async_copy(
        psi_ref.at[:, pl.ds(pl.multiple_of(k * rb, rb), rb)], vec.at[mine], local_sem.at[1]
    )
    own_r = pltpu.make_async_copy(right_ref.at[:, k], r_all.at[z], local_sem.at[0])
    own_e = pltpu.make_async_copy(env_ref, env, local_sem.at[2])
    own_l.start()
    own_p.start()
    own_r.start()
    own_e.start()

    own_l.wait()
    diff = lax.broadcasted_iota(jnp.int32, (bs, all_rows), 1) - lax.broadcasted_iota(
        jnp.int32, (bs, all_rows), 0
    )
    for t in range(terms):
        for d in range(nd):
            total = jnp.zeros((bs, all_rows), F32)
            for j in range(nnz):
                place = jnp.where(diff == bs * src_ref[t, d, j], 1.0, 0.0).astype(BF16)
                total += jnp.dot(left[t, d, j], place, preferred_element_type=F32)
            at = pl.ds(pl.multiple_of(c * rows + d * bs, bs), bs)
            l_all[z, t, at, :] = total.astype(BF16)

    pl.semaphore_wait(barrier, n + 2)

    def hop(ref, way, o, h, step, send, recv):
        to = lax.rem(z + 1, n) if way == 0 else lax.rem(z + n - 1, n)
        return remote(ref(o, h), ref(o, h), send.at[way, step, h], recv.at[o, h], {"op": to})

    def start_line(ref, send, recv, pieces):
        for h in pieces:
            @pl.when(z + 1 < n)
            def _():
                hop(ref, 0, z, h, 0, send, recv).start()

            @pl.when(z > 0)
            def _():
                hop(ref, 1, z, h, 0, send, recv).start()

    def step_line(ref, send, recv, s, pieces, use):
        for h in pieces:
            @pl.when(z - s >= 0)
            def _():
                o = lax.rem(z - s + n, n)
                hop(ref, 0, o, h, 0, send, recv).wait_recv()
                if s < n - 1:
                    @pl.when(z + 1 < n)
                    def _():
                        hop(ref, 0, o, h, s, send, recv).start()
                use(o, h)

            @pl.when(z + s < n)
            def _():
                o = lax.rem(z + s, n)
                hop(ref, 1, o, h, 0, send, recv).wait_recv()
                if s < n - 1:
                    @pl.when(z > 0)
                    def _():
                        hop(ref, 1, o, h, s, send, recv).start()
                use(o, h)

    def arrived(s, use):
        @pl.when(z - s >= 0)
        def _():
            use(lax.rem(z - s + n, n))

        @pl.when(z + s < n)
        def _():
            use(lax.rem(z + s, n))

    def end_line(ref, send, recv, pieces):
        for s in range(n - 1):
            for h in pieces:
                @pl.when((z + 1 < n) & (z - s >= 0))
                def _():
                    hop(ref, 0, lax.rem(z - s + n, n), h, s, send, recv).wait_send()

                @pl.when((z > 0) & (z + s < n))
                def _():
                    hop(ref, 1, lax.rem(z + s, n), h, s, send, recv).wait_send()

    def l_slot(o, t):
        return l_all.at[o, t, mine, :]

    def to_sibling(o, t):
        return remote(l_slot(o, t), l_slot(o, t), s_send.at[o, t], s_recv.at[o, t], sibling)

    def partner(i):
        falling = jnp.where(n - 1 - i > z, n - 1 - i, n - 2 - i)
        rising = jnp.where(i >= z, i + 1, i)
        return lax.rem(jnp.where(z < n // 2, falling, rising) + n, n)

    def r_copy(i, t):
        dest = partner(i)
        return remote(
            right_ref.at[t, 2 * dest + c], r_all.at[z, t], r_send.at[i, t], r_recv.at[z, t],
            {"op": dest},
        )

    every = range(terms)
    start_line(l_slot, l_send, l_recv, every)
    p_copy = remote(
        psi_ref.at[:, pl.ds(pl.multiple_of(ksib * rb, rb), rb)], vec.at[mine],
        p_send, p_recv, sibling,
    )
    p_copy.start()
    for t in every:
        to_sibling(z, t).start()
    work = [(i, t) for i in range(n - 1) for t in every]
    share = [len(work) * s // n for s in range(1, n)]
    done = 0
    for s in range(1, n):
        for i, t in work[done:share[s - 1]]:
            r_copy(i, t).start()
        done = share[s - 1]
        step_line(l_slot, l_send, l_recv, s, every, lambda o, t: to_sibling(o, t).start())
    for i, t in work[done:]:
        r_copy(i, t).start()

    own_p.wait()
    p_copy.wait()
    own_r.wait()

    def product(o, t):
        moved = jnp.dot(vec[...], r_all[o, t], preferred_element_type=F32).astype(BF16)
        return jnp.dot(l_all[o, t], moved, preferred_element_type=F32)

    image = jnp.zeros((all_rows, rb), F32)
    for i in range(-1, n - 1):
        o = z if i < 0 else partner(i)
        for t in every:
            to_sibling(o, t).wait_recv()
            if i >= 0:
                remote(
                    right_ref.at[t, k], r_all.at[o, t], r_send.at[0, 0], r_recv.at[o, t],
                    {"op": o},
                ).wait_recv()
            image = image + product(o, t)

    exponent = jnp.zeros((1, 1), F32)

    def settle(image, exponent):
        top = jnp.max(jnp.abs(image), axis=(0, 1), keepdims=True)
        e = jnp.where(top > 0.0, jnp.clip(jnp.floor(jnp.log2(top)), -100.0, 100.0), 0.0)
        return image * jnp.exp2(-e), exponent + e

    for step in range(1, ITERS):
        image, exponent = settle(image, exponent)
        vec[...] = image.astype(BF16)
        image = jnp.zeros((all_rows, rb), F32)
        for o in range(n):
            for t in every:
                image = image + product(o, t)
    image, exponent = settle(image, exponent)
    vec[...] = image.astype(BF16)

    x_copy = remote(vec.at[theirs, :], tail.at[z, c], x_send.at[0], x_recv.at[0], sibling)
    x_copy.start()
    tail[z, c] = vec[mine, :]

    def a_slot(o, h):
        return tail.at[o, c if h == 0 else 1 - c]

    start_line(a_slot, a_send, a_recv, (0,))
    square = jnp.sum(image * image, axis=(0, 1), keepdims=True)
    lane = lax.broadcasted_iota(jnp.int32, (8, 128), 1)
    meta[z, c] = jnp.where(lane == 0, jnp.broadcast_to(exponent, (8, 128)),
                           jnp.broadcast_to(square, (8, 128)))
    xm_copy = remote(meta.at[z, c], meta.at[z, c], x_send.at[1], x_recv.at[1], sibling)
    xm_copy.start()
    x_copy.wait()
    start_line(a_slot, a_send, a_recv, (1,))
    xm_copy.wait()

    def m_copy(off):
        return remote(
            meta.at[z], meta.at[z], m_send.at[off], m_recv.at[z], {"op": lax.rem(z + off, n)}
        )

    for off in range(1, n):
        m_copy(off).start()

    step_line(a_slot, a_send, a_recv, 1, (0, 1), lambda o, h: None)
    for off in range(1, n):
        o = lax.rem(z + off, n)
        remote(
            meta.at[o], meta.at[o], m_send.at[0], m_recv.at[o], {"op": o}
        ).wait_recv()

    exps = [meta[o // 2, o % 2][0:1, 0:1] for o in range(2 * n)]
    sqs = [meta[o // 2, o % 2][0:1, 1:2] for o in range(2 * n)]
    low = jnp.full((1, 1), -1.0e4, F32)
    big = low
    for e, q in zip(exps, sqs):
        big = jnp.maximum(big, jnp.where(q > 0.0, e, low))
    ww = jnp.zeros((1, 1), F32)
    weights = []
    for e, q in zip(exps, sqs):
        r = jnp.where(q > 0.0, jnp.exp2(jnp.maximum(e - big, -120.0)), 0.0)
        weights.append(r)
        ww = ww + q * r * r
    unit = jnp.sqrt(float(all_rows * cols) / ww)
    for o, r in enumerate(weights):
        rel[o] = jnp.broadcast_to(r * unit, (8, 128))

    own_e.wait()
    total_fac[...] = jnp.zeros(out_ref.shape, F32)

    def finish(o):
        part = total_fac[...]
        for half in range(2):
            scale = rel[2 * o + half][0:1, 0:1]
            block = (tail[o, half].astype(F32) * scale).astype(BF16)
            at = pl.ds(pl.multiple_of((2 * o + half) * rb, rb), rb)
            amp_ref[:, at] = block
            part = part + jnp.dot(block, env[at, :], preferred_element_type=F32)
        total_fac[...] = part

    finish(z)
    arrived(1, finish)
    for s in range(2, n):
        step_line(a_slot, a_send, a_recv, s, (0, 1), lambda o, h: None)
        arrived(s, finish)

    fac[...] = total_fac[...].astype(BF16)
    f_copy = remote(fac, fac_in, f_send, f_recv, across)
    f_copy.start()
    rounded = fac[...].astype(F32)
    fsq = jnp.sum(rounded * rounded, axis=(0, 1), keepdims=True)
    fmeta[0] = jnp.broadcast_to(fsq, (8, 128))
    g_near = remote(fmeta.at[0], fmeta.at[1], g_send.at[0], g_recv.at[0], across)
    g_far = remote(fmeta.at[0], fmeta.at[2], g_send.at[1], g_recv.at[1], diagonal)
    g_near.start()
    g_far.start()

    for i, t in work:
        r_copy(i, t).wait_send()
    for off in range(1, n):
        m_copy(off).wait_send()
    end_line(l_slot, l_send, l_recv, every)
    end_line(a_slot, a_send, a_recv, (0, 1))
    for o in range(n):
        for t in every:
            to_sibling(o, t).wait_send()
    eye = jnp.where(
        lax.broadcasted_iota(jnp.int32, out_ref.shape, 0) + c * rows
        == lax.broadcasted_iota(jnp.int32, out_ref.shape, 1), 1.0, 0.0,
    )
    first = jnp.full(out_ref.shape, site, jnp.int32) == 0
    g_near.wait()
    g_far.wait()
    f_copy.wait()
    total = fmeta[1][0:1, 0:1] + fmeta[2][0:1, 0:1]
    earlier = fac_in[...].astype(F32) * lax.rsqrt(total / float(all_rows * out_ref.shape[1]))
    out_ref[...] = jnp.where(first, eye, earlier)


def column_plan(psi, right_ops, left_blocks, sources, env_basis):
    n = lax.axis_size("op")
    rows, cols = psi.shape[1], psi.shape[2]
    terms, nrb, rb = right_ops.shape[1], right_ops.shape[2], right_ops.shape[3]
    width = env_basis.shape[2]
    dma = pltpu.SemaphoreType.DMA
    hbm = pl.BlockSpec(memory_space=pltpu.HBM)
    vmem = pl.BlockSpec(memory_space=pltpu.VMEM)
    amplitudes, environment = pl.pallas_call(
        functools.partial(column_kernel, n),
        out_shape=(
            jax.ShapeDtypeStruct((rows, cols), BF16),
            jax.ShapeDtypeStruct((rows, width), F32),
        ),
        in_specs=[pl.BlockSpec(memory_space=pltpu.SMEM), hbm, hbm, hbm, hbm],
        out_specs=(vmem, vmem),
        scratch_shapes=[
            pltpu.VMEM((n, terms, rb, rb), BF16),
            pltpu.VMEM((n, terms, 2 * rows, 2 * rows), BF16),
            pltpu.VMEM((2 * rows, rb), BF16),
            pltpu.VMEM((cols, width), BF16),
            pltpu.VMEM(left_blocks.shape[1:], BF16),
            pltpu.VMEM((n, 2, rows, rb), BF16),
            pltpu.VMEM((n, 2, 8, 128), F32),
            pltpu.VMEM((2 * n, 8, 128), F32),
            pltpu.VMEM((rows, width), F32),
            pltpu.VMEM((rows, width), BF16),
            pltpu.VMEM((rows, width), BF16),
            pltpu.VMEM((3, 8, 128), F32),
            dma((4,)),
            dma((n, terms)), dma((n, terms)), dma, dma,
            dma((2, n, terms)), dma((n, terms)), dma((n, terms)), dma((n, terms)),
            dma((2, n, 2)), dma((n, 2)), dma((2,)), dma((2,)), dma((n,)), dma((n,)),
            dma, dma, dma((2,)), dma((2,)),
        ],
        compiler_params=pltpu.CompilerParams(
            collective_id=0, has_side_effects=True, vmem_limit_bytes=53 * 1024 * 1024
        ),
    )(sources[0], psi[0], right_ops[0], left_blocks[0], env_basis[0])
    return (amplitudes[None], environment[None])


def on_device(psi, right_ops, left_blocks, sources, env_basis):
    owners = lax.axis_size("op") * lax.axis_size("blk")
    fits = (
        owners == right_ops.shape[2]
        and lax.axis_size("blk") == 2
        and lax.axis_size("site") == 2
        and psi.shape[0] == 1
        and env_basis.shape[2] == 2 * psi.shape[1]
    )
    plan = column_plan if fits else general_plan
    return plan(psi, right_ops, left_blocks, sources, env_basis)


def solution(mesh):
    placed = (
        P(("group", "site"), "blk", None),
        P(("group", "site"), "op", None, None, None),
        P(("group", "site"), "op", "blk", None, None, None),
        P(("group", "site"), "op", "blk", None),
        P(("group", "site"), None, None),
    )
    return jax.shard_map(
        on_device,
        mesh=mesh,
        in_specs=placed,
        out_specs=(P(("group", "site"), "blk", None), P(("group", "site"), "blk", None)),
        check_vma=False,
    )
```

```python
import functools

import jax
import jax.numpy as jnp
from jax import lax
from jax.experimental import pallas as pl
from jax.experimental.pallas import tpu as pltpu
from jax.sharding import PartitionSpec as P

ITERS = 3
MESH = pl.DeviceIdType.MESH
F32 = jnp.float32
BF16 = jnp.bfloat16


def entering(value, axis, combine, identity):
    size, here = (lax.axis_size(axis), lax.axis_index(axis))
    everything = lax.all_gather(value.astype(jnp.bfloat16), axis)
    start = jnp.broadcast_to(jnp.asarray(identity, value.dtype), value.shape)

    def lap(k, before):
        reached = k < here
        new = combine(before, everything[k].astype(value.dtype))
        return jnp.where(reached, new, before)

    return lax.fori_loop(0, size, lap, start)


def chain_product(first, second):
    return jnp.dot(
        first, second, precision=lax.Precision.HIGHEST, preferred_element_type=jnp.float32
    )


def pick_rows(table, index):
    return table[index]


def local_terms(vector, right_seg, left_seg, source_seg):
    local_rows, cols = vector.shape
    nrb, rblock = (right_seg.shape[1], right_seg.shape[2])
    bsize = left_seg.shape[-1]
    split = vector.reshape(local_rows, nrb, rblock)
    moved = jnp.einsum("ikb,tkbc->tikc", split, right_seg, preferred_element_type=jnp.float32)
    moved = moved.reshape(right_seg.shape[0], local_rows, cols).astype(jnp.bfloat16)
    gathered = lax.all_gather(moved, "blk", axis=1, tiled=True)
    stacked = gathered.reshape(gathered.shape[0], gathered.shape[1] // bsize, bsize, cols)
    picked = jax.vmap(pick_rows)(stacked, source_seg)
    image = jnp.einsum("tdjab,tdjbc->dac", left_seg, picked, preferred_element_type=jnp.float32)
    return image.reshape(local_rows, cols)


def general_plan(psi, right_ops, left_blocks, sources, env_basis):
    local_rows, cols = (psi.shape[1], psi.shape[2])
    count = float(local_rows * lax.axis_size("blk") * cols)
    vector = psi[0]
    for step in range(ITERS):
        partial_sum = local_terms(vector, right_ops[0], left_blocks[0], sources[0])
        image = lax.psum(partial_sum, "op")
        inner_ww = lax.psum(jnp.sum(image * image), "blk")
        vector = (image * jnp.sqrt(count / inner_ww)).astype(jnp.bfloat16)
    factor_rows = jnp.dot(vector, env_basis[0], preferred_element_type=jnp.float32)
    factor = lax.all_gather(factor_rows.astype(jnp.bfloat16), "blk", axis=0, tiled=True).astype(
        factor_rows.dtype
    )
    total_rows = factor.shape[1]
    factor = factor * jnp.sqrt(float(total_rows * total_rows) / jnp.sum(factor * factor))
    identity = jnp.eye(total_rows, dtype=jnp.float32)
    carried = entering(factor, "site", chain_product, identity)
    scaled = carried * lax.rsqrt(jnp.mean(carried * carried))
    settled = jnp.where(lax.axis_index("site") == 0, carried, scaled)
    mine = lax.dynamic_slice_in_dim(settled, lax.axis_index("blk") * local_rows, local_rows, 0)
    return (vector[None], mine[None])


def column_kernel(
    n, src_ref, psi_ref, right_ref, left_ref, env_ref, amp_ref, out_ref,
    src, r_all, l_all, vec, env, left, tail, meta, rel, total_fac, fac, fac_in, fmeta,
    local_sem, r_send, r_recv, p_send, p_recv, l_send, l_recv, s_send, s_recv,
    a_send, a_recv, x_send, x_recv, m_send, m_recv, f_send, f_recv, g_send, g_recv,
):
    terms, nrb, rb, _ = right_ref.shape
    rows, cols = psi_ref.shape
    nd, nnz, bs = left_ref.shape[1], left_ref.shape[2], left_ref.shape[3]
    all_rows = 2 * rows
    z = lax.axis_index("op")
    c = lax.axis_index("blk")
    site = lax.axis_index("site")
    k = 2 * z + c
    ksib = 2 * z + 1 - c
    mine = pl.ds(pl.multiple_of(c * rows, rows), rows)
    theirs = pl.ds(pl.multiple_of((1 - c) * rows, rows), rows)

    def remote(src, dst, send, recv, device):
        return pltpu.make_async_remote_copy(
            src_ref=src, dst_ref=dst, send_sem=send, recv_sem=recv,
            device_id=device, device_id_type=MESH,
        )

    sibling = {"blk": 1 - c}
    across = {"site": 1 - site}
    diagonal = {"site": 1 - site, "blk": 1 - c}

    barrier = pltpu.get_barrier_semaphore()
    for off in range(1, n):
        pl.semaphore_signal(
            barrier, inc=1, device_id={"op": lax.rem(z + off, n)}, device_id_type=MESH
        )
    for dev in (sibling, across, diagonal):
        pl.semaphore_signal(barrier, inc=1, device_id=dev, device_id_type=MESH)

    own_l = pltpu.make_async_copy(left_ref, left, local_sem.at[3])
    own_p = pltpu.make_async_copy(
        psi_ref.at[:, pl.ds(pl.multiple_of(k * rb, rb), rb)], vec.at[mine], local_sem.at[1]
    )
    own_r = pltpu.make_async_copy(right_ref.at[:, k], r_all.at[z], local_sem.at[0])
    own_e = pltpu.make_async_copy(env_ref, env, local_sem.at[2])
    own_s = pltpu.make_async_copy(src_ref, src, local_sem.at[4])
    own_s.start()
    own_l.start()
    own_p.start()
    own_r.start()
    own_e.start()

    own_s.wait()
    own_l.wait()
    diff = lax.broadcasted_iota(jnp.int32, (bs, all_rows), 1) - lax.broadcasted_iota(
        jnp.int32, (bs, all_rows), 0
    )
    for t in range(terms):
        for d in range(nd):
            total = jnp.zeros((bs, all_rows), F32)
            for j in range(nnz):
                place = jnp.where(diff == bs * src[t, d, j], 1.0, 0.0).astype(BF16)
                total += jnp.dot(left[t, d, j], place, preferred_element_type=F32)
            at = pl.ds(pl.multiple_of(c * rows + d * bs, bs), bs)
            l_all[z, t, at, :] = total.astype(BF16)

    pl.semaphore_wait(barrier, n + 2)

    def hop(ref, way, o, h, step, send, recv):
        to = lax.rem(z + 1, n) if way == 0 else lax.rem(z + n - 1, n)
        return remote(ref(o, h), ref(o, h), send.at[way, step, h], recv.at[o, h], {"op": to})

    def start_line(ref, send, recv, pieces):
        for h in pieces:
            @pl.when(z + 1 < n)
            def _():
                hop(ref, 0, z, h, 0, send, recv).start()

            @pl.when(z > 0)
            def _():
                hop(ref, 1, z, h, 0, send, recv).start()

    def step_line(ref, send, recv, s, pieces, use):
        for h in pieces:
            @pl.when(z - s >= 0)
            def _():
                o = lax.rem(z - s + n, n)
                hop(ref, 0, o, h, 0, send, recv).wait_recv()
                if s < n - 1:
                    @pl.when(z + 1 < n)
                    def _():
                        hop(ref, 0, o, h, s, send, recv).start()
                use(o, h)

            @pl.when(z + s < n)
            def _():
                o = lax.rem(z + s, n)
                hop(ref, 1, o, h, 0, send, recv).wait_recv()
                if s < n - 1:
                    @pl.when(z > 0)
                    def _():
                        hop(ref, 1, o, h, s, send, recv).start()
                use(o, h)

    def arrived(s, use):
        @pl.when(z - s >= 0)
        def _():
            use(lax.rem(z - s + n, n))

        @pl.when(z + s < n)
        def _():
            use(lax.rem(z + s, n))

    def end_line(ref, send, recv, pieces):
        for s in range(n - 1):
            for h in pieces:
                @pl.when((z + 1 < n) & (z - s >= 0))
                def _():
                    hop(ref, 0, lax.rem(z - s + n, n), h, s, send, recv).wait_send()

                @pl.when((z > 0) & (z + s < n))
                def _():
                    hop(ref, 1, lax.rem(z + s, n), h, s, send, recv).wait_send()

    def l_slot(o, t):
        return l_all.at[o, t, mine, :]

    def to_sibling(o, t):
        return remote(l_slot(o, t), l_slot(o, t), s_send.at[o, t], s_recv.at[o, t], sibling)

    def partner(i):
        falling = jnp.where(n - 1 - i > z, n - 1 - i, n - 2 - i)
        rising = jnp.where(i >= z, i + 1, i)
        return lax.rem(jnp.where(z < n // 2, falling, rising) + n, n)

    def r_copy(i, t):
        dest = partner(i)
        return remote(
            right_ref.at[t, 2 * dest + c], r_all.at[z, t], r_send.at[i, t], r_recv.at[z, t],
            {"op": dest},
        )

    every = range(terms)
    start_line(l_slot, l_send, l_recv, every)
    p_copy = remote(
        psi_ref.at[:, pl.ds(pl.multiple_of(ksib * rb, rb), rb)], vec.at[mine],
        p_send, p_recv, sibling,
    )
    p_copy.start()
    for t in every:
        to_sibling(z, t).start()
    work = [(i, t) for t in every for i in range(n - 1)]
    share = [len(work) * s // n for s in range(1, n)]
    done = 0
    for s in range(1, n):
        for i, t in work[done:share[s - 1]]:
            r_copy(i, t).start()
        done = share[s - 1]
        step_line(l_slot, l_send, l_recv, s, every, lambda o, t: to_sibling(o, t).start())
    for i, t in work[done:]:
        r_copy(i, t).start()

    own_p.wait()
    p_copy.wait()
    own_r.wait()

    def product(o, t):
        moved = jnp.dot(vec[...], r_all[o, t], preferred_element_type=F32).astype(BF16)
        return jnp.dot(l_all[o, t], moved, preferred_element_type=F32)

    image = jnp.zeros((all_rows, rb), F32)
    for i in range(-1, n - 1):
        o = z if i < 0 else partner(i)
        for t in every:
            to_sibling(o, t).wait_recv()
            if i >= 0:
                remote(
                    right_ref.at[t, k], r_all.at[o, t], r_send.at[0, 0], r_recv.at[o, t],
                    {"op": o},
                ).wait_recv()
            image = image + product(o, t)

    exponent = jnp.zeros((1, 1), F32)

    def settle(image, exponent):
        top = jnp.max(jnp.abs(image), axis=(0, 1), keepdims=True)
        e = jnp.where(top > 0.0, jnp.clip(jnp.floor(jnp.log2(top)), -100.0, 100.0), 0.0)
        return image * jnp.exp2(-e), exponent + e

    for step in range(1, ITERS):
        image, exponent = settle(image, exponent)
        vec[...] = image.astype(BF16)
        image = jnp.zeros((all_rows, rb), F32)
        v = vec[...]
        for o in range(n):
            moved = [jnp.dot(v, r_all[o, t], preferred_element_type=F32).astype(BF16)
                     for t in every]
            image = image + jnp.dot(
                jnp.concatenate([l_all[o, t] for t in every], axis=1),
                jnp.concatenate(moved, axis=0), preferred_element_type=F32)
    image, exponent = settle(image, exponent)
    vec[...] = image.astype(BF16)

    x_copy = remote(vec.at[theirs, :], tail.at[z, c], x_send.at[0], x_recv.at[0], sibling)
    x_copy.start()
    tail[z, c] = vec[mine, :]

    def a_slot(o, h):
        return tail.at[o, c if h == 0 else 1 - c]

    start_line(a_slot, a_send, a_recv, (0,))
    square = jnp.sum(image * image, axis=(0, 1), keepdims=True)
    lane = lax.broadcasted_iota(jnp.int32, (8, 128), 1)
    meta[z, c] = jnp.where(lane == 0, jnp.broadcast_to(exponent, (8, 128)),
                           jnp.broadcast_to(square, (8, 128)))
    xm_copy = remote(meta.at[z, c], meta.at[z, c], x_send.at[1], x_recv.at[1], sibling)
    xm_copy.start()
    x_copy.wait()
    start_line(a_slot, a_send, a_recv, (1,))
    xm_copy.wait()

    def m_copy(off):
        return remote(
            meta.at[z], meta.at[z], m_send.at[off], m_recv.at[z], {"op": lax.rem(z + off, n)}
        )

    for off in range(1, n):
        m_copy(off).start()

    step_line(a_slot, a_send, a_recv, 1, (0, 1), lambda o, h: None)
    for off in range(1, n):
        o = lax.rem(z + off, n)
        remote(
            meta.at[o], meta.at[o], m_send.at[0], m_recv.at[o], {"op": o}
        ).wait_recv()

    exps = [meta[o // 2, o % 2][0:1, 0:1] for o in range(2 * n)]
    sqs = [meta[o // 2, o % 2][0:1, 1:2] for o in range(2 * n)]
    low = jnp.full((1, 1), -1.0e4, F32)
    big = low
    for e, q in zip(exps, sqs):
        big = jnp.maximum(big, jnp.where(q > 0.0, e, low))
    ww = jnp.zeros((1, 1), F32)
    weights = []
    for e, q in zip(exps, sqs):
        r = jnp.where(q > 0.0, jnp.exp2(jnp.maximum(e - big, -120.0)), 0.0)
        weights.append(r)
        ww = ww + q * r * r
    unit = jnp.sqrt(float(all_rows * cols) / ww)
    for o, r in enumerate(weights):
        rel[o] = jnp.broadcast_to(r * unit, (8, 128))

    own_e.wait()
    total_fac[...] = jnp.zeros(out_ref.shape, F32)

    def finish(o):
        part = total_fac[...]
        for half in range(2):
            scale = rel[2 * o + half][0:1, 0:1]
            block = (tail[o, half].astype(F32) * scale).astype(BF16)
            at = pl.ds(pl.multiple_of((2 * o + half) * rb, rb), rb)
            amp_ref[:, at] = block
            part = part + jnp.dot(block, env[at, :], preferred_element_type=F32)
        total_fac[...] = part

    finish(z)
    arrived(1, finish)
    for s in range(2, n):
        step_line(a_slot, a_send, a_recv, s, (0, 1), lambda o, h: None)
        arrived(s, finish)

    fac[...] = total_fac[...].astype(BF16)
    f_copy = remote(fac, fac_in, f_send, f_recv, across)
    f_copy.start()
    rounded = fac[...].astype(F32)
    fsq = jnp.sum(rounded * rounded, axis=(0, 1), keepdims=True)
    fmeta[0] = jnp.broadcast_to(fsq, (8, 128))
    g_near = remote(fmeta.at[0], fmeta.at[1], g_send.at[0], g_recv.at[0], across)
    g_far = remote(fmeta.at[0], fmeta.at[2], g_send.at[1], g_recv.at[1], diagonal)
    g_near.start()
    g_far.start()

    for i, t in work:
        r_copy(i, t).wait_send()
    for off in range(1, n):
        m_copy(off).wait_send()
    end_line(l_slot, l_send, l_recv, every)
    end_line(a_slot, a_send, a_recv, (0, 1))
    for o in range(n):
        for t in every:
            to_sibling(o, t).wait_send()
    eye = jnp.where(
        lax.broadcasted_iota(jnp.int32, out_ref.shape, 0) + c * rows
        == lax.broadcasted_iota(jnp.int32, out_ref.shape, 1), 1.0, 0.0,
    )
    first = jnp.full(out_ref.shape, site, jnp.int32) == 0
    g_near.wait()
    g_far.wait()
    f_copy.wait()
    total = fmeta[1][0:1, 0:1] + fmeta[2][0:1, 0:1]
    earlier = fac_in[...].astype(F32) * lax.rsqrt(total / float(all_rows * out_ref.shape[1]))
    out_ref[...] = jnp.where(first, eye, earlier)


def column_plan(psi, right_ops, left_blocks, sources, env_basis):
    n = lax.axis_size("op")
    rows, cols = psi.shape[1], psi.shape[2]
    terms, nrb, rb = right_ops.shape[1], right_ops.shape[2], right_ops.shape[3]
    width = env_basis.shape[2]
    dma = pltpu.SemaphoreType.DMA
    hbm = pl.BlockSpec(memory_space=pltpu.HBM)
    vmem = pl.BlockSpec(memory_space=pltpu.VMEM)
    amplitudes, environment = pl.pallas_call(
        functools.partial(column_kernel, n),
        out_shape=(
            jax.ShapeDtypeStruct((rows, cols), BF16),
            jax.ShapeDtypeStruct((rows, width), F32),
        ),
        in_specs=[hbm, hbm, hbm, hbm, hbm],
        out_specs=(vmem, vmem),
        scratch_shapes=[
            pltpu.SMEM(sources.shape[1:], jnp.int32),
            pltpu.VMEM((n, terms, rb, rb), BF16),
            pltpu.VMEM((n, terms, 2 * rows, 2 * rows), BF16),
            pltpu.VMEM((2 * rows, rb), BF16),
            pltpu.VMEM((cols, width), BF16),
            pltpu.VMEM(left_blocks.shape[1:], BF16),
            pltpu.VMEM((n, 2, rows, rb), BF16),
            pltpu.VMEM((n, 2, 8, 128), F32),
            pltpu.VMEM((2 * n, 8, 128), F32),
            pltpu.VMEM((rows, width), F32),
            pltpu.VMEM((rows, width), BF16),
            pltpu.VMEM((rows, width), BF16),
            pltpu.VMEM((3, 8, 128), F32),
            dma((5,)),
            dma((n, terms)), dma((n, terms)), dma, dma,
            dma((2, n, terms)), dma((n, terms)), dma((n, terms)), dma((n, terms)),
            dma((2, n, 2)), dma((n, 2)), dma((2,)), dma((2,)), dma((n,)), dma((n,)),
            dma, dma, dma((2,)), dma((2,)),
        ],
        compiler_params=pltpu.CompilerParams(
            collective_id=0, has_side_effects=True, vmem_limit_bytes=53 * 1024 * 1024
        ),
    )(sources[0], psi[0], right_ops[0], left_blocks[0], env_basis[0])
    return (amplitudes[None], environment[None])


def on_device(psi, right_ops, left_blocks, sources, env_basis):
    owners = lax.axis_size("op") * lax.axis_size("blk")
    fits = (
        owners == right_ops.shape[2]
        and lax.axis_size("blk") == 2
        and lax.axis_size("site") == 2
        and psi.shape[0] == 1
        and env_basis.shape[2] == 2 * psi.shape[1]
    )
    plan = column_plan if fits else general_plan
    return plan(psi, right_ops, left_blocks, sources, env_basis)


def solution(mesh):
    placed = (
        P(("group", "site"), "blk", None),
        P(("group", "site"), "op", None, None, None),
        P(("group", "site"), "op", "blk", None, None, None),
        P(("group", "site"), "op", "blk", None),
        P(("group", "site"), None, None),
    )
    return jax.shard_map(
        on_device,
        mesh=mesh,
        in_specs=placed,
        out_specs=(P(("group", "site"), "blk", None), P(("group", "site"), "blk", None)),
        check_vma=False,
    )
```

```python
import functools

import jax
import jax.numpy as jnp
from jax import lax
from jax.experimental import pallas as pl
from jax.experimental.pallas import tpu as pltpu
from jax.sharding import PartitionSpec as P

ITERS = 3
MESH = pl.DeviceIdType.MESH
F32 = jnp.float32
BF16 = jnp.bfloat16


def entering(value, axis, combine, identity):
    size, here = (lax.axis_size(axis), lax.axis_index(axis))
    everything = lax.all_gather(value.astype(jnp.bfloat16), axis)
    start = jnp.broadcast_to(jnp.asarray(identity, value.dtype), value.shape)

    def lap(k, before):
        reached = k < here
        new = combine(before, everything[k].astype(value.dtype))
        return jnp.where(reached, new, before)

    return lax.fori_loop(0, size, lap, start)


def chain_product(first, second):
    return jnp.dot(
        first, second, precision=lax.Precision.HIGHEST, preferred_element_type=jnp.float32
    )


def pick_rows(table, index):
    return table[index]


def local_terms(vector, right_seg, left_seg, source_seg):
    local_rows, cols = vector.shape
    nrb, rblock = (right_seg.shape[1], right_seg.shape[2])
    bsize = left_seg.shape[-1]
    split = vector.reshape(local_rows, nrb, rblock)
    moved = jnp.einsum("ikb,tkbc->tikc", split, right_seg, preferred_element_type=jnp.float32)
    moved = moved.reshape(right_seg.shape[0], local_rows, cols).astype(jnp.bfloat16)
    gathered = lax.all_gather(moved, "blk", axis=1, tiled=True)
    stacked = gathered.reshape(gathered.shape[0], gathered.shape[1] // bsize, bsize, cols)
    picked = jax.vmap(pick_rows)(stacked, source_seg)
    image = jnp.einsum("tdjab,tdjbc->dac", left_seg, picked, preferred_element_type=jnp.float32)
    return image.reshape(local_rows, cols)


def general_plan(psi, right_ops, left_blocks, sources, env_basis):
    local_rows, cols = (psi.shape[1], psi.shape[2])
    count = float(local_rows * lax.axis_size("blk") * cols)
    vector = psi[0]
    for step in range(ITERS):
        partial_sum = local_terms(vector, right_ops[0], left_blocks[0], sources[0])
        image = lax.psum(partial_sum, "op")
        inner_ww = lax.psum(jnp.sum(image * image), "blk")
        vector = (image * jnp.sqrt(count / inner_ww)).astype(jnp.bfloat16)
    factor_rows = jnp.dot(vector, env_basis[0], preferred_element_type=jnp.float32)
    factor = lax.all_gather(factor_rows.astype(jnp.bfloat16), "blk", axis=0, tiled=True).astype(
        factor_rows.dtype
    )
    total_rows = factor.shape[1]
    factor = factor * jnp.sqrt(float(total_rows * total_rows) / jnp.sum(factor * factor))
    identity = jnp.eye(total_rows, dtype=jnp.float32)
    carried = entering(factor, "site", chain_product, identity)
    scaled = carried * lax.rsqrt(jnp.mean(carried * carried))
    settled = jnp.where(lax.axis_index("site") == 0, carried, scaled)
    mine = lax.dynamic_slice_in_dim(settled, lax.axis_index("blk") * local_rows, local_rows, 0)
    return (vector[None], mine[None])


def column_kernel(
    n, src_ref, psi_ref, right_ref, left_ref, env_ref, amp_ref, out_ref,
    src, r_all, l_all, vec, env, left, tail, meta, rel, total_fac, fac, fac_in, fmeta,
    local_sem, r_send, r_recv, p_send, p_recv, l_send, l_recv, s_send, s_recv,
    a_send, a_recv, x_send, x_recv, m_send, m_recv, f_send, f_recv, g_send, g_recv,
):
    terms, nrb, rb, _ = right_ref.shape
    rows, cols = psi_ref.shape
    nd, nnz, bs = left_ref.shape[1], left_ref.shape[2], left_ref.shape[3]
    all_rows = 2 * rows
    z = lax.axis_index("op")
    c = lax.axis_index("blk")
    site = lax.axis_index("site")
    k = 2 * z + c
    ksib = 2 * z + 1 - c
    mine = pl.ds(pl.multiple_of(c * rows, rows), rows)
    theirs = pl.ds(pl.multiple_of((1 - c) * rows, rows), rows)

    def remote(src, dst, send, recv, device):
        return pltpu.make_async_remote_copy(
            src_ref=src, dst_ref=dst, send_sem=send, recv_sem=recv,
            device_id=device, device_id_type=MESH,
        )

    sibling = {"blk": 1 - c}
    across = {"site": 1 - site}
    diagonal = {"site": 1 - site, "blk": 1 - c}

    barrier = pltpu.get_barrier_semaphore()
    for off in range(1, n):
        pl.semaphore_signal(
            barrier, inc=1, device_id={"op": lax.rem(z + off, n)}, device_id_type=MESH
        )
    for dev in (sibling, across, diagonal):
        pl.semaphore_signal(barrier, inc=1, device_id=dev, device_id_type=MESH)

    own_l = pltpu.make_async_copy(left_ref, left, local_sem.at[3])
    own_p = pltpu.make_async_copy(
        psi_ref.at[:, pl.ds(pl.multiple_of(k * rb, rb), rb)], vec.at[mine], local_sem.at[1]
    )
    own_r = pltpu.make_async_copy(right_ref.at[:, k], r_all.at[z], local_sem.at[0])
    own_e = pltpu.make_async_copy(env_ref, env, local_sem.at[2])
    own_s = pltpu.make_async_copy(src_ref, src, local_sem.at[4])
    own_s.start()
    own_l.start()
    own_p.start()
    own_r.start()
    own_e.start()

    own_s.wait()
    own_l.wait()
    diff = lax.broadcasted_iota(jnp.int32, (bs, all_rows), 1) - lax.broadcasted_iota(
        jnp.int32, (bs, all_rows), 0
    )
    for t in range(terms):
        for d in range(nd):
            total = jnp.zeros((bs, all_rows), F32)
            for j in range(nnz):
                place = jnp.where(diff == bs * src[t, d, j], 1.0, 0.0).astype(BF16)
                total += jnp.dot(left[t, d, j], place, preferred_element_type=F32)
            at = pl.ds(pl.multiple_of(c * rows + d * bs, bs), bs)
            l_all[z, t, at, :] = total.astype(BF16)

    pl.semaphore_wait(barrier, n + 2)

    def hop(ref, way, o, h, step, send, recv):
        to = lax.rem(z + 1, n) if way == 0 else lax.rem(z + n - 1, n)
        return remote(ref(o, h), ref(o, h), send.at[way, step, h], recv.at[o, h], {"op": to})

    def start_line(ref, send, recv, pieces):
        for h in pieces:
            @pl.when(z + 1 < n)
            def _():
                hop(ref, 0, z, h, 0, send, recv).start()

            @pl.when(z > 0)
            def _():
                hop(ref, 1, z, h, 0, send, recv).start()

    def step_line(ref, send, recv, s, pieces, use):
        for h in pieces:
            @pl.when(z - s >= 0)
            def _():
                o = lax.rem(z - s + n, n)
                hop(ref, 0, o, h, 0, send, recv).wait_recv()
                if s < n - 1:
                    @pl.when(z + 1 < n)
                    def _():
                        hop(ref, 0, o, h, s, send, recv).start()
                use(o, h)

            @pl.when(z + s < n)
            def _():
                o = lax.rem(z + s, n)
                hop(ref, 1, o, h, 0, send, recv).wait_recv()
                if s < n - 1:
                    @pl.when(z > 0)
                    def _():
                        hop(ref, 1, o, h, s, send, recv).start()
                use(o, h)

    def arrived(s, use):
        @pl.when(z - s >= 0)
        def _():
            use(lax.rem(z - s + n, n))

        @pl.when(z + s < n)
        def _():
            use(lax.rem(z + s, n))

    def end_line(ref, send, recv, pieces):
        for s in range(n - 1):
            for h in pieces:
                @pl.when((z + 1 < n) & (z - s >= 0))
                def _():
                    hop(ref, 0, lax.rem(z - s + n, n), h, s, send, recv).wait_send()

                @pl.when((z > 0) & (z + s < n))
                def _():
                    hop(ref, 1, lax.rem(z + s, n), h, s, send, recv).wait_send()

    def l_slot(o, t):
        return l_all.at[o, t, mine, :]

    def to_sibling(o, t):
        return remote(l_slot(o, t), l_slot(o, t), s_send.at[o, t], s_recv.at[o, t], sibling)

    def partner(i):
        falling = jnp.where(n - 1 - i > z, n - 1 - i, n - 2 - i)
        rising = jnp.where(i >= z, i + 1, i)
        return lax.rem(jnp.where(z < n // 2, falling, rising) + n, n)

    def r_copy(i, t):
        dest = partner(i)
        return remote(
            right_ref.at[t, 2 * dest + c], r_all.at[z, t], r_send.at[i, t], r_recv.at[z, t],
            {"op": dest},
        )

    every = range(terms)
    start_line(l_slot, l_send, l_recv, every)
    p_copy = remote(
        psi_ref.at[:, pl.ds(pl.multiple_of(ksib * rb, rb), rb)], vec.at[mine],
        p_send, p_recv, sibling,
    )
    p_copy.start()
    for t in every:
        to_sibling(z, t).start()
    work = [(i, t) for t in every for i in range(n - 1)]
    share = [len(work) * s // n for s in range(1, n)]
    done = 0
    for s in range(1, n):
        for i, t in work[done:share[s - 1]]:
            r_copy(i, t).start()
        done = share[s - 1]
        step_line(l_slot, l_send, l_recv, s, every, lambda o, t: to_sibling(o, t).start())
    for i, t in work[done:]:
        r_copy(i, t).start()

    own_p.wait()
    p_copy.wait()
    own_r.wait()

    def product(o, t):
        moved = jnp.dot(vec[...], r_all[o, t], preferred_element_type=F32).astype(BF16)
        return jnp.dot(l_all[o, t], moved, preferred_element_type=F32)

    image = jnp.zeros((all_rows, rb), F32)
    for i in range(-1, n - 1):
        o = z if i < 0 else partner(i)
        for t in every:
            to_sibling(o, t).wait_recv()
            if i >= 0:
                remote(
                    right_ref.at[t, k], r_all.at[o, t], r_send.at[0, 0], r_recv.at[o, t],
                    {"op": o},
                ).wait_recv()
            image = image + product(o, t)

    exponent = jnp.zeros((1, 1), F32)

    def settle(image, exponent):
        top = jnp.max(jnp.abs(image), axis=(0, 1), keepdims=True)
        e = jnp.where(top > 0.0, jnp.clip(jnp.floor(jnp.log2(top)), -100.0, 100.0), 0.0)
        return image * jnp.exp2(-e), exponent + e

    for step in range(1, ITERS):
        image, exponent = settle(image, exponent)
        vec[...] = image.astype(BF16)
        image = jnp.zeros((all_rows, rb), F32)
        v = vec[...]
        for o in range(n):
            moved = [jnp.dot(v, r_all[o, t], preferred_element_type=F32).astype(BF16)
                     for t in every]
            image = image + jnp.dot(
                jnp.concatenate([l_all[o, t] for t in every], axis=1),
                jnp.concatenate(moved, axis=0), preferred_element_type=F32)
    image, exponent = settle(image, exponent)
    vec[...] = image.astype(BF16)

    x_copy = remote(vec.at[theirs, :], tail.at[z, c], x_send.at[0], x_recv.at[0], sibling)
    x_copy.start()
    tail[z, c] = vec[mine, :]

    def a_slot(o, h):
        return tail.at[o, c if h < 2 else 1 - c, pl.ds((h % 2) * (rows // 2), rows // 2)]

    start_line(a_slot, a_send, a_recv, (0, 1))
    square = jnp.sum(image * image, axis=(0, 1), keepdims=True)
    lane = lax.broadcasted_iota(jnp.int32, (8, 128), 1)
    meta[z, c] = jnp.where(lane == 0, jnp.broadcast_to(exponent, (8, 128)),
                           jnp.broadcast_to(square, (8, 128)))
    xm_copy = remote(meta.at[z, c], meta.at[z, c], x_send.at[1], x_recv.at[1], sibling)
    xm_copy.start()
    x_copy.wait()
    start_line(a_slot, a_send, a_recv, (2, 3))
    xm_copy.wait()

    def m_copy(off):
        return remote(
            meta.at[z], meta.at[z], m_send.at[off], m_recv.at[z], {"op": lax.rem(z + off, n)}
        )

    for off in range(1, n):
        m_copy(off).start()

    step_line(a_slot, a_send, a_recv, 1, range(4), lambda o, h: None)
    for off in range(1, n):
        o = lax.rem(z + off, n)
        remote(
            meta.at[o], meta.at[o], m_send.at[0], m_recv.at[o], {"op": o}
        ).wait_recv()

    exps = [meta[o // 2, o % 2][0:1, 0:1] for o in range(2 * n)]
    sqs = [meta[o // 2, o % 2][0:1, 1:2] for o in range(2 * n)]
    low = jnp.full((1, 1), -1.0e4, F32)
    big = low
    for e, q in zip(exps, sqs):
        big = jnp.maximum(big, jnp.where(q > 0.0, e, low))
    ww = jnp.zeros((1, 1), F32)
    weights = []
    for e, q in zip(exps, sqs):
        r = jnp.where(q > 0.0, jnp.exp2(jnp.maximum(e - big, -120.0)), 0.0)
        weights.append(r)
        ww = ww + q * r * r
    unit = jnp.sqrt(float(all_rows * cols) / ww)
    for o, r in enumerate(weights):
        rel[o] = jnp.broadcast_to(r * unit, (8, 128))

    own_e.wait()
    total_fac[...] = jnp.zeros(out_ref.shape, F32)

    def finish(o):
        part = total_fac[...]
        for half in range(2):
            scale = rel[2 * o + half][0:1, 0:1]
            block = (tail[o, half].astype(F32) * scale).astype(BF16)
            at = pl.ds(pl.multiple_of((2 * o + half) * rb, rb), rb)
            amp_ref[:, at] = block
            part = part + jnp.dot(block, env[at, :], preferred_element_type=F32)
        total_fac[...] = part

    finish(z)
    arrived(1, finish)
    for s in range(2, n):
        step_line(a_slot, a_send, a_recv, s, range(4), lambda o, h: None)
        arrived(s, finish)

    fac[...] = total_fac[...].astype(BF16)
    f_copy = remote(fac, fac_in, f_send, f_recv, across)
    f_copy.start()
    rounded = fac[...].astype(F32)
    fsq = jnp.sum(rounded * rounded, axis=(0, 1), keepdims=True)
    fmeta[0] = jnp.broadcast_to(fsq, (8, 128))
    g_near = remote(fmeta.at[0], fmeta.at[1], g_send.at[0], g_recv.at[0], across)
    g_far = remote(fmeta.at[0], fmeta.at[2], g_send.at[1], g_recv.at[1], diagonal)
    g_near.start()
    g_far.start()

    for i, t in work:
        r_copy(i, t).wait_send()
    for off in range(1, n):
        m_copy(off).wait_send()
    end_line(l_slot, l_send, l_recv, every)
    end_line(a_slot, a_send, a_recv, range(4))
    for o in range(n):
        for t in every:
            to_sibling(o, t).wait_send()
    eye = jnp.where(
        lax.broadcasted_iota(jnp.int32, out_ref.shape, 0) + c * rows
        == lax.broadcasted_iota(jnp.int32, out_ref.shape, 1), 1.0, 0.0,
    )
    first = jnp.full(out_ref.shape, site, jnp.int32) == 0
    g_near.wait()
    g_far.wait()
    f_copy.wait()
    total = fmeta[1][0:1, 0:1] + fmeta[2][0:1, 0:1]
    earlier = fac_in[...].astype(F32) * lax.rsqrt(total / float(all_rows * out_ref.shape[1]))
    out_ref[...] = jnp.where(first, eye, earlier)


def column_plan(psi, right_ops, left_blocks, sources, env_basis):
    n = lax.axis_size("op")
    rows, cols = psi.shape[1], psi.shape[2]
    terms, nrb, rb = right_ops.shape[1], right_ops.shape[2], right_ops.shape[3]
    width = env_basis.shape[2]
    dma = pltpu.SemaphoreType.DMA
    hbm = pl.BlockSpec(memory_space=pltpu.HBM)
    vmem = pl.BlockSpec(memory_space=pltpu.VMEM)
    amplitudes, environment = pl.pallas_call(
        functools.partial(column_kernel, n),
        out_shape=(
            jax.ShapeDtypeStruct((rows, cols), BF16),
            jax.ShapeDtypeStruct((rows, width), F32),
        ),
        in_specs=[hbm, hbm, hbm, hbm, hbm],
        out_specs=(vmem, vmem),
        scratch_shapes=[
            pltpu.SMEM(sources.shape[1:], jnp.int32),
            pltpu.VMEM((n, terms, rb, rb), BF16),
            pltpu.VMEM((n, terms, 2 * rows, 2 * rows), BF16),
            pltpu.VMEM((2 * rows, rb), BF16),
            pltpu.VMEM((cols, width), BF16),
            pltpu.VMEM(left_blocks.shape[1:], BF16),
            pltpu.VMEM((n, 2, rows, rb), BF16),
            pltpu.VMEM((n, 2, 8, 128), F32),
            pltpu.VMEM((2 * n, 8, 128), F32),
            pltpu.VMEM((rows, width), F32),
            pltpu.VMEM((rows, width), BF16),
            pltpu.VMEM((rows, width), BF16),
            pltpu.VMEM((3, 8, 128), F32),
            dma((5,)),
            dma((n, terms)), dma((n, terms)), dma, dma,
            dma((2, n, terms)), dma((n, terms)), dma((n, terms)), dma((n, terms)),
            dma((2, n, 4)), dma((n, 4)), dma((2,)), dma((2,)), dma((n,)), dma((n,)),
            dma, dma, dma((2,)), dma((2,)),
        ],
        compiler_params=pltpu.CompilerParams(
            collective_id=0, has_side_effects=True, vmem_limit_bytes=53 * 1024 * 1024
        ),
    )(sources[0], psi[0], right_ops[0], left_blocks[0], env_basis[0])
    return (amplitudes[None], environment[None])


def on_device(psi, right_ops, left_blocks, sources, env_basis):
    owners = lax.axis_size("op") * lax.axis_size("blk")
    fits = (
        owners == right_ops.shape[2]
        and lax.axis_size("blk") == 2
        and lax.axis_size("site") == 2
        and psi.shape[0] == 1
        and env_basis.shape[2] == 2 * psi.shape[1]
    )
    plan = column_plan if fits else general_plan
    return plan(psi, right_ops, left_blocks, sources, env_basis)


def solution(mesh):
    placed = (
        P(("group", "site"), "blk", None),
        P(("group", "site"), "op", None, None, None),
        P(("group", "site"), "op", "blk", None, None, None),
        P(("group", "site"), "op", "blk", None),
        P(("group", "site"), None, None),
    )
    return jax.shard_map(
        on_device,
        mesh=mesh,
        in_specs=placed,
        out_specs=(P(("group", "site"), "blk", None), P(("group", "site"), "blk", None)),
        check_vma=False,
    )
```

```python
import functools

import jax
import jax.numpy as jnp
from jax import lax
from jax.experimental import pallas as pl
from jax.experimental.pallas import tpu as pltpu
from jax.sharding import PartitionSpec as P

ITERS = 3
MESH = pl.DeviceIdType.MESH
F32 = jnp.float32
BF16 = jnp.bfloat16


def entering(value, axis, combine, identity):
    size, here = (lax.axis_size(axis), lax.axis_index(axis))
    everything = lax.all_gather(value.astype(jnp.bfloat16), axis)
    start = jnp.broadcast_to(jnp.asarray(identity, value.dtype), value.shape)

    def lap(k, before):
        reached = k < here
        new = combine(before, everything[k].astype(value.dtype))
        return jnp.where(reached, new, before)

    return lax.fori_loop(0, size, lap, start)


def chain_product(first, second):
    return jnp.dot(
        first, second, precision=lax.Precision.HIGHEST, preferred_element_type=jnp.float32
    )


def pick_rows(table, index):
    return table[index]


def local_terms(vector, right_seg, left_seg, source_seg):
    local_rows, cols = vector.shape
    nrb, rblock = (right_seg.shape[1], right_seg.shape[2])
    bsize = left_seg.shape[-1]
    split = vector.reshape(local_rows, nrb, rblock)
    moved = jnp.einsum("ikb,tkbc->tikc", split, right_seg, preferred_element_type=jnp.float32)
    moved = moved.reshape(right_seg.shape[0], local_rows, cols).astype(jnp.bfloat16)
    gathered = lax.all_gather(moved, "blk", axis=1, tiled=True)
    stacked = gathered.reshape(gathered.shape[0], gathered.shape[1] // bsize, bsize, cols)
    picked = jax.vmap(pick_rows)(stacked, source_seg)
    image = jnp.einsum("tdjab,tdjbc->dac", left_seg, picked, preferred_element_type=jnp.float32)
    return image.reshape(local_rows, cols)


def general_plan(psi, right_ops, left_blocks, sources, env_basis):
    local_rows, cols = (psi.shape[1], psi.shape[2])
    count = float(local_rows * lax.axis_size("blk") * cols)
    vector = psi[0]
    for step in range(ITERS):
        partial_sum = local_terms(vector, right_ops[0], left_blocks[0], sources[0])
        image = lax.psum(partial_sum, "op")
        inner_ww = lax.psum(jnp.sum(image * image), "blk")
        vector = (image * jnp.sqrt(count / inner_ww)).astype(jnp.bfloat16)
    factor_rows = jnp.dot(vector, env_basis[0], preferred_element_type=jnp.float32)
    factor = lax.all_gather(factor_rows.astype(jnp.bfloat16), "blk", axis=0, tiled=True).astype(
        factor_rows.dtype
    )
    total_rows = factor.shape[1]
    factor = factor * jnp.sqrt(float(total_rows * total_rows) / jnp.sum(factor * factor))
    identity = jnp.eye(total_rows, dtype=jnp.float32)
    carried = entering(factor, "site", chain_product, identity)
    scaled = carried * lax.rsqrt(jnp.mean(carried * carried))
    settled = jnp.where(lax.axis_index("site") == 0, carried, scaled)
    mine = lax.dynamic_slice_in_dim(settled, lax.axis_index("blk") * local_rows, local_rows, 0)
    return (vector[None], mine[None])


def column_kernel(
    n, src_ref, psi_ref, right_ref, left_ref, env_ref, amp_ref, out_ref,
    src, r_all, l_all, vec, env, left, tail, meta, rel, total_fac, fac, fac_in, fmeta,
    local_sem, r_send, r_recv, p_send, p_recv, l_send, l_recv, s_send, s_recv,
    a_send, a_recv, x_send, x_recv, m_send, m_recv, f_send, f_recv, g_send, g_recv,
):
    terms, nrb, rb, _ = right_ref.shape
    rows, cols = psi_ref.shape
    nd, nnz, bs = left_ref.shape[1], left_ref.shape[2], left_ref.shape[3]
    all_rows = 2 * rows
    z = lax.axis_index("op")
    c = lax.axis_index("blk")
    site = lax.axis_index("site")
    k = 2 * z + c
    ksib = 2 * z + 1 - c
    mine = pl.ds(pl.multiple_of(c * rows, rows), rows)
    theirs = pl.ds(pl.multiple_of((1 - c) * rows, rows), rows)

    def remote(src, dst, send, recv, device):
        return pltpu.make_async_remote_copy(
            src_ref=src, dst_ref=dst, send_sem=send, recv_sem=recv,
            device_id=device, device_id_type=MESH,
        )

    sibling = {"blk": 1 - c}
    across = {"site": 1 - site}
    diagonal = {"site": 1 - site, "blk": 1 - c}

    barrier = pltpu.get_barrier_semaphore()
    for off in range(1, n):
        pl.semaphore_signal(
            barrier, inc=1, device_id={"op": lax.rem(z + off, n)}, device_id_type=MESH
        )
    for dev in (sibling, across, diagonal):
        pl.semaphore_signal(barrier, inc=1, device_id=dev, device_id_type=MESH)

    own_l = pltpu.make_async_copy(left_ref, left, local_sem.at[3])
    own_p = pltpu.make_async_copy(
        psi_ref.at[:, pl.ds(pl.multiple_of(k * rb, rb), rb)], vec.at[mine], local_sem.at[1]
    )
    own_r = pltpu.make_async_copy(right_ref.at[:, k], r_all.at[z], local_sem.at[0])
    own_e = pltpu.make_async_copy(env_ref, env, local_sem.at[2])
    own_s = pltpu.make_async_copy(src_ref, src, local_sem.at[4])
    own_s.start()
    own_l.start()
    own_p.start()
    own_r.start()
    own_e.start()

    own_s.wait()
    own_l.wait()
    diff = lax.broadcasted_iota(jnp.int32, (bs, all_rows), 1) - lax.broadcasted_iota(
        jnp.int32, (bs, all_rows), 0
    )
    for t in range(terms):
        for d in range(nd):
            total = jnp.zeros((bs, all_rows), F32)
            for j in range(nnz):
                place = jnp.where(diff == bs * src[t, d, j], 1.0, 0.0).astype(BF16)
                total += jnp.dot(left[t, d, j], place, preferred_element_type=F32)
            at = pl.ds(pl.multiple_of(c * rows + d * bs, bs), bs)
            l_all[z, t, at, :] = total.astype(BF16)

    pl.semaphore_wait(barrier, n + 2)

    def hop(ref, way, o, h, step, send, recv):
        to = lax.rem(z + 1, n) if way == 0 else lax.rem(z + n - 1, n)
        return remote(ref(o, h), ref(o, h), send.at[way, step, h], recv.at[o, h], {"op": to})

    def start_line(ref, send, recv, pieces):
        for h in pieces:
            @pl.when(z + 1 < n)
            def _():
                hop(ref, 0, z, h, 0, send, recv).start()

            @pl.when(z > 0)
            def _():
                hop(ref, 1, z, h, 0, send, recv).start()

    def step_line(ref, send, recv, s, pieces, use):
        for h in pieces:
            @pl.when(z - s >= 0)
            def _():
                o = lax.rem(z - s + n, n)
                hop(ref, 0, o, h, 0, send, recv).wait_recv()
                if s < n - 1:
                    @pl.when(z + 1 < n)
                    def _():
                        hop(ref, 0, o, h, s, send, recv).start()
                use(o, h)

            @pl.when(z + s < n)
            def _():
                o = lax.rem(z + s, n)
                hop(ref, 1, o, h, 0, send, recv).wait_recv()
                if s < n - 1:
                    @pl.when(z > 0)
                    def _():
                        hop(ref, 1, o, h, s, send, recv).start()
                use(o, h)

    def arrived(s, use):
        @pl.when(z - s >= 0)
        def _():
            use(lax.rem(z - s + n, n))

        @pl.when(z + s < n)
        def _():
            use(lax.rem(z + s, n))

    def end_line(ref, send, recv, pieces):
        for s in range(n - 1):
            for h in pieces:
                @pl.when((z + 1 < n) & (z - s >= 0))
                def _():
                    hop(ref, 0, lax.rem(z - s + n, n), h, s, send, recv).wait_send()

                @pl.when((z > 0) & (z + s < n))
                def _():
                    hop(ref, 1, lax.rem(z + s, n), h, s, send, recv).wait_send()

    def l_slot(o, t):
        return l_all.at[o, t, mine, :]

    def to_sibling(o, t):
        return remote(l_slot(o, t), l_slot(o, t), s_send.at[o, t], s_recv.at[o, t], sibling)

    def partner(i):
        falling = jnp.where(n - 1 - i > z, n - 1 - i, n - 2 - i)
        rising = jnp.where(i >= z, i + 1, i)
        return lax.rem(jnp.where(z < n // 2, falling, rising) + n, n)

    def r_copy(i, t):
        dest = partner(i)
        return remote(
            right_ref.at[t, 2 * dest + c], r_all.at[z, t], r_send.at[i, t], r_recv.at[z, t],
            {"op": dest},
        )

    every = range(terms)
    start_line(l_slot, l_send, l_recv, every)
    p_copy = remote(
        psi_ref.at[:, pl.ds(pl.multiple_of(ksib * rb, rb), rb)], vec.at[mine],
        p_send, p_recv, sibling,
    )
    p_copy.start()
    for t in every:
        to_sibling(z, t).start()
    work = [(i, t) for t in every for i in range(n - 1)]
    share = [len(work) * s // n for s in range(1, n)]
    done = 0
    for s in range(1, n):
        for i, t in work[done:share[s - 1]]:
            r_copy(i, t).start()
        done = share[s - 1]
        step_line(l_slot, l_send, l_recv, s, every, lambda o, t: to_sibling(o, t).start())
    for i, t in work[done:]:
        r_copy(i, t).start()

    own_p.wait()
    p_copy.wait()
    own_r.wait()

    def product(o, t):
        moved = jnp.dot(vec[...], r_all[o, t], preferred_element_type=F32).astype(BF16)
        return jnp.dot(l_all[o, t], moved, preferred_element_type=F32)

    image = jnp.zeros((all_rows, rb), F32)
    for i in range(-1, n - 1):
        o = z if i < 0 else partner(i)
        for t in every:
            to_sibling(o, t).wait_recv()
            if i >= 0:
                remote(
                    right_ref.at[t, k], r_all.at[o, t], r_send.at[0, 0], r_recv.at[o, t],
                    {"op": o},
                ).wait_recv()
            image = image + product(o, t)

    exponent = jnp.zeros((1, 1), F32)

    def settle(image, exponent):
        top = jnp.max(jnp.abs(image), axis=(0, 1), keepdims=True)
        e = jnp.where(top > 0.0, jnp.clip(jnp.floor(jnp.log2(top)), -100.0, 100.0), 0.0)
        return image * jnp.exp2(-e), exponent + e

    for step in range(1, ITERS):
        image, exponent = settle(image, exponent)
        vec[...] = image.astype(BF16)
        v = vec[...]
        moved = [jnp.dot(v, r_all[o, t], preferred_element_type=F32).astype(BF16)
                 for o in range(n) for t in every]
        image = jnp.dot(
            jnp.concatenate([l_all[o, t] for o in range(n) for t in every], axis=1),
            jnp.concatenate(moved, axis=0), preferred_element_type=F32)
    image, exponent = settle(image, exponent)
    vec[...] = image.astype(BF16)

    x_copy = remote(vec.at[theirs, :], tail.at[z, c], x_send.at[0], x_recv.at[0], sibling)
    x_copy.start()
    tail[z, c] = vec[mine, :]

    def a_slot(o, h):
        return tail.at[o, c if h < 2 else 1 - c, pl.ds((h % 2) * (rows // 2), rows // 2)]

    start_line(a_slot, a_send, a_recv, (0, 1))
    square = jnp.sum(image * image, axis=(0, 1), keepdims=True)
    lane = lax.broadcasted_iota(jnp.int32, (8, 128), 1)
    meta[z, c] = jnp.where(lane == 0, jnp.broadcast_to(exponent, (8, 128)),
                           jnp.broadcast_to(square, (8, 128)))
    xm_copy = remote(meta.at[z, c], meta.at[z, c], x_send.at[1], x_recv.at[1], sibling)
    xm_copy.start()
    x_copy.wait()
    start_line(a_slot, a_send, a_recv, (2, 3))
    xm_copy.wait()

    def m_copy(off):
        return remote(
            meta.at[z], meta.at[z], m_send.at[off], m_recv.at[z], {"op": lax.rem(z + off, n)}
        )

    for off in range(1, n):
        m_copy(off).start()

    step_line(a_slot, a_send, a_recv, 1, range(4), lambda o, h: None)
    for off in range(1, n):
        o = lax.rem(z + off, n)
        remote(
            meta.at[o], meta.at[o], m_send.at[0], m_recv.at[o], {"op": o}
        ).wait_recv()

    exps = [meta[o // 2, o % 2][0:1, 0:1] for o in range(2 * n)]
    sqs = [meta[o // 2, o % 2][0:1, 1:2] for o in range(2 * n)]
    low = jnp.full((1, 1), -1.0e4, F32)
    big = low
    for e, q in zip(exps, sqs):
        big = jnp.maximum(big, jnp.where(q > 0.0, e, low))
    ww = jnp.zeros((1, 1), F32)
    weights = []
    for e, q in zip(exps, sqs):
        r = jnp.where(q > 0.0, jnp.exp2(jnp.maximum(e - big, -120.0)), 0.0)
        weights.append(r)
        ww = ww + q * r * r
    unit = jnp.sqrt(float(all_rows * cols) / ww)
    for o, r in enumerate(weights):
        rel[o] = jnp.broadcast_to(r * unit, (8, 128))

    own_e.wait()
    total_fac[...] = jnp.zeros(out_ref.shape, F32)

    def finish(o):
        part = total_fac[...]
        for half in range(2):
            scale = rel[2 * o + half][0:1, 0:1]
            block = (tail[o, half].astype(F32) * scale).astype(BF16)
            at = pl.ds(pl.multiple_of((2 * o + half) * rb, rb), rb)
            amp_ref[:, at] = block
            part = part + jnp.dot(block, env[at, :], preferred_element_type=F32)
        total_fac[...] = part

    finish(z)
    arrived(1, finish)
    for s in range(2, n):
        step_line(a_slot, a_send, a_recv, s, range(4), lambda o, h: None)
        arrived(s, finish)

    fac[...] = total_fac[...].astype(BF16)
    f_copy = remote(fac, fac_in, f_send, f_recv, across)
    f_copy.start()
    rounded = fac[...].astype(F32)
    fsq = jnp.sum(rounded * rounded, axis=(0, 1), keepdims=True)
    fmeta[0] = jnp.broadcast_to(fsq, (8, 128))
    g_near = remote(fmeta.at[0], fmeta.at[1], g_send.at[0], g_recv.at[0], across)
    g_far = remote(fmeta.at[0], fmeta.at[2], g_send.at[1], g_recv.at[1], diagonal)
    g_near.start()
    g_far.start()

    for i, t in work:
        r_copy(i, t).wait_send()
    for off in range(1, n):
        m_copy(off).wait_send()
    end_line(l_slot, l_send, l_recv, every)
    end_line(a_slot, a_send, a_recv, range(4))
    for o in range(n):
        for t in every:
            to_sibling(o, t).wait_send()
    eye = jnp.where(
        lax.broadcasted_iota(jnp.int32, out_ref.shape, 0) + c * rows
        == lax.broadcasted_iota(jnp.int32, out_ref.shape, 1), 1.0, 0.0,
    )
    first = jnp.full(out_ref.shape, site, jnp.int32) == 0
    g_near.wait()
    g_far.wait()
    f_copy.wait()
    total = fmeta[1][0:1, 0:1] + fmeta[2][0:1, 0:1]
    earlier = fac_in[...].astype(F32) * lax.rsqrt(total / float(all_rows * out_ref.shape[1]))
    out_ref[...] = jnp.where(first, eye, earlier)


def column_plan(psi, right_ops, left_blocks, sources, env_basis):
    n = lax.axis_size("op")
    rows, cols = psi.shape[1], psi.shape[2]
    terms, nrb, rb = right_ops.shape[1], right_ops.shape[2], right_ops.shape[3]
    width = env_basis.shape[2]
    dma = pltpu.SemaphoreType.DMA
    hbm = pl.BlockSpec(memory_space=pltpu.HBM)
    vmem = pl.BlockSpec(memory_space=pltpu.VMEM)
    amplitudes, environment = pl.pallas_call(
        functools.partial(column_kernel, n),
        out_shape=(
            jax.ShapeDtypeStruct((rows, cols), BF16),
            jax.ShapeDtypeStruct((rows, width), F32),
        ),
        in_specs=[hbm, hbm, hbm, hbm, hbm],
        out_specs=(vmem, vmem),
        scratch_shapes=[
            pltpu.SMEM(sources.shape[1:], jnp.int32),
            pltpu.VMEM((n, terms, rb, rb), BF16),
            pltpu.VMEM((n, terms, 2 * rows, 2 * rows), BF16),
            pltpu.VMEM((2 * rows, rb), BF16),
            pltpu.VMEM((cols, width), BF16),
            pltpu.VMEM(left_blocks.shape[1:], BF16),
            pltpu.VMEM((n, 2, rows, rb), BF16),
            pltpu.VMEM((n, 2, 8, 128), F32),
            pltpu.VMEM((2 * n, 8, 128), F32),
            pltpu.VMEM((rows, width), F32),
            pltpu.VMEM((rows, width), BF16),
            pltpu.VMEM((rows, width), BF16),
            pltpu.VMEM((3, 8, 128), F32),
            dma((5,)),
            dma((n, terms)), dma((n, terms)), dma, dma,
            dma((2, n, terms)), dma((n, terms)), dma((n, terms)), dma((n, terms)),
            dma((2, n, 4)), dma((n, 4)), dma((2,)), dma((2,)), dma((n,)), dma((n,)),
            dma, dma, dma((2,)), dma((2,)),
        ],
        compiler_params=pltpu.CompilerParams(
            collective_id=0, has_side_effects=True, vmem_limit_bytes=53 * 1024 * 1024
        ),
    )(sources[0], psi[0], right_ops[0], left_blocks[0], env_basis[0])
    return (amplitudes[None], environment[None])


def on_device(psi, right_ops, left_blocks, sources, env_basis):
    owners = lax.axis_size("op") * lax.axis_size("blk")
    fits = (
        owners == right_ops.shape[2]
        and lax.axis_size("blk") == 2
        and lax.axis_size("site") == 2
        and psi.shape[0] == 1
        and env_basis.shape[2] == 2 * psi.shape[1]
    )
    plan = column_plan if fits else general_plan
    return plan(psi, right_ops, left_blocks, sources, env_basis)


def solution(mesh):
    placed = (
        P(("group", "site"), "blk", None),
        P(("group", "site"), "op", None, None, None),
        P(("group", "site"), "op", "blk", None, None, None),
        P(("group", "site"), "op", "blk", None),
        P(("group", "site"), None, None),
    )
    return jax.shard_map(
        on_device,
        mesh=mesh,
        in_specs=placed,
        out_specs=(P(("group", "site"), "blk", None), P(("group", "site"), "blk", None)),
        check_vma=False,
    )
```
